256 devices in a mesh: head: 4 (over z_lo, core), inner: 4 (over z_hi), outer: 16 (over y, x).
Axes of the slice: x: 4, y: 4, z: 8 (z_hi: 4, z_lo: 2; z = z_hi * 2 + z_lo), core: 2. Of those that a mesh axis runs over, the one named last changes fastest.
Arguments:
- query: bfloat16 [64, 192, 16, 128], P(('inner', 'outer'), 'head'), may hold values from -8 to 8
- key_in: bfloat16 [64, 192, 16, 128], P(('inner', 'outer'), 'head'), may hold values from -8 to 8
- value: bfloat16 [64, 192, 16, 128], P(('inner', 'outer'), 'head'), may hold values from -6 to 6
- doc_ids: int32 [12288], P(('inner', 'outer')), may hold values from 0 to 7, never falling along the last dimension, each value on 1 to 6144 neighbouring positions
- out_weight: bfloat16 [2048, 4096], P('head'), may hold values from -0.25 to 0.25
Outputs:
- mixed: bfloat16 [64, 192, 4096], P(('inner', 'outer'), 'head')
The draws below stay inside these ranges and needn't reach their ends.
Inputs may be any that keep to these rules, and one draw needn't show every extreme that they name: `doc_ids`: record numbers never fall along the tokens; a record may span up to 6144 positions.
All inputs are finite; a program needn't handle non-finite values.
Results may differ from the reference program's by a relative error of at most 0.012.
Values may be sent and summed in bfloat16 or wider, within the bound.
No kernel may reach another device: no remote copies, remote signals or barrier semaphores. Data moves between devices by JAX's collectives and lax.ppermute only.
A program may use at most 192 MiB of HBM per device.

```python
import math
import jax
import jax.numpy as jnp
import numpy as np
from jax import lax

D = 4096
H = 16
HD = 128
CTX_DEV = 192
DOCS = 8
CTXN = 64
TOKENS = 12288


def draw_query(key, part):
    key = jax.random.fold_in(key, 11)
    base = jnp.clip(1.5 * jax.random.normal(key, (TOKENS, H, HD), jnp.float32), -8.0, 8.0)
    return base.reshape(CTXN, CTX_DEV, H, HD).astype(jnp.bfloat16)


def draw_key_in(key, part):
    key = jax.random.fold_in(key, 23)
    base = jnp.clip(jax.random.normal(key, (TOKENS, H, HD), jnp.float32), -8.0, 8.0)
    return base.reshape(CTXN, CTX_DEV, H, HD).astype(jnp.bfloat16)


def block_levels(stream_key, extent, pieces, low, top_value):
    loudness = 1.0
    for axis_at, parts in pieces:
        heights = jax.random.uniform(jax.random.fold_in(jax.random.fold_in(stream_key, 6), axis_at), (parts,), jnp.float32, low / len(pieces), top_value / len(pieces))
        loudness = loudness * jnp.repeat(jnp.exp(heights), extent[axis_at] // parts).reshape((-1,) + (1,) * (len(extent) - 1 - axis_at))
    return loudness


def length_profile(count, total, limit, lean):
    loads = [(1 << 20) // math.isqrt(rank ** lean) + 1 for rank in range(2, count + 1)]
    spare, given = total - limit - (count - 1), [1] * (count - 1)
    while spare > 0:
        movable = [i for i in range(count - 1) if given[i] < limit]
        whole, budget = sum([loads[i] for i in movable]), spare
        for i in movable:
            more = min(limit - given[i], max(1, budget * loads[i] // whole), spare)
            given[i] = given[i] + more
            spare = spare - more
    return np.array([limit] + given)


def uneven_parts(own_key, number_of, total, limit, lean):
    if number_of == 2:
        one = jax.random.randint(own_key, (), max(1, total - limit), min(limit, total - 1) + 1)
        return jnp.stack([one, total - one])
    sizes = jnp.asarray(length_profile(number_of, total, limit, lean), jnp.int32)
    couples = (number_of - 1) // 2
    source_of, sink = sizes[1:1 + 2 * couples:2], sizes[2:2 + 2 * couples:2]
    slack = jnp.minimum(source_of - 1, limit - sink)
    moved = jax.random.randint(jax.random.fold_in(own_key, 1), (couples,), 0, 1 << 20) % (slack + 1)
    sizes = sizes.at[1:1 + 2 * couples:2].set(source_of - moved).at[2:2 + 2 * couples:2].set(sink + moved)
    return sizes[jax.random.permutation(jax.random.fold_in(own_key, 2), number_of)]


def gaussian(rng, extent, width, most, pieces=(), held_as=jnp.bfloat16):
    drawn = width * jax.random.normal(rng, extent, jnp.float32)
    if pieces:
        drawn = drawn * block_levels(rng, extent, pieces, -0.22, 0.18)
    return jnp.clip(drawn, -most, most).astype(held_as)


def setup_inputs(seed: int = 0) -> dict:
    key_of = jax.random.split(jax.random.key(seed), 6)
    query = draw_query(jax.random.fold_in(key_of[5], 71), 0)
    key_in = draw_key_in(jax.random.fold_in(key_of[5], 71), 0)
    value = gaussian(key_of[2], (CTXN, CTX_DEV, H, HD), 1.0, 6.0, ((0, 64), (1, 4)))
    doc_ids = jnp.searchsorted(jnp.cumsum(uneven_parts(key_of[3], DOCS, TOKENS, TOKENS // 2, 1)), jnp.arange(TOKENS), side="right").astype(jnp.int32)
    out_weight = gaussian(key_of[4], (H * HD, D), (H * HD // 4) ** -0.5, 0.25, ((0, 4),))
    return dict(query=query, key_in=key_in, value=value, doc_ids=doc_ids, out_weight=out_weight)


def reference(query, key_in, value, doc_ids, out_weight):
    token_count = query.shape[0] * query.shape[1]
    queries = query.reshape(token_count, H, HD)
    keys_all = key_in.reshape(token_count, H, HD)
    values_all = value.reshape(token_count, H, HD)
    positions = jnp.arange(token_count, dtype=jnp.int32)
    block_size = math.gcd(token_count, 512)
    block_count = token_count // block_size
    scaling = 1.0 / math.sqrt(HD)

    def one_head(head_index):
        q_head = lax.dynamic_index_in_dim(queries, head_index, 1, keepdims=False)
        k_head = lax.dynamic_index_in_dim(keys_all, head_index, 1, keepdims=False)
        v_head = lax.dynamic_index_in_dim(values_all, head_index, 1, keepdims=False)

        def one_block(block_index):
            row_start = (block_index * block_size).astype(jnp.int32)
            row_block = lax.dynamic_slice_in_dim(q_head, row_start, block_size, 0)
            row_positions = lax.dynamic_slice_in_dim(positions, row_start, block_size, 0)
            row_docs = lax.dynamic_slice_in_dim(doc_ids, row_start, block_size, 0)
            scores = jnp.dot(row_block, k_head.T, preferred_element_type=jnp.float32) * scaling
            allowed = (positions[None, :] <= row_positions[:, None]) & (doc_ids[None, :] == row_docs[:, None])
            scores = jnp.where(allowed, scores, -jnp.inf)
            row_max = lax.optimization_barrier(jnp.max(scores, axis=-1, keepdims=True))
            weights = jnp.exp(scores - row_max)
            denominator = lax.optimization_barrier(jnp.sum(weights, axis=-1, keepdims=True))
            numerator = jnp.dot(weights.astype(jnp.bfloat16), v_head, preferred_element_type=jnp.float32)
            return (numerator / denominator).astype(jnp.bfloat16)
        outputs = lax.map(one_block, jnp.arange(block_count, dtype=jnp.int32))
        return outputs.reshape(token_count, HD)
    heads_out = lax.map(one_head, jnp.arange(H, dtype=jnp.int32))
    attended = heads_out.transpose(1, 0, 2).reshape(token_count, H * HD)
    mixed = jnp.dot(attended, out_weight, preferred_element_type=jnp.float32).astype(jnp.bfloat16)
    return mixed.reshape(query.shape[0], query.shape[1], out_weight.shape[1])
```

```python
import functools
import itertools
import math

import jax
import jax.numpy as jnp
from jax import lax
from jax.experimental import pallas as pl
from jax.experimental.pallas import tpu as pltpu
from jax.sharding import Mesh
from jax.sharding import PartitionSpec as P

SIZES = {"zl": 2, "core": 2, "zh": 4, "y": 4, "x": 4}
AXES = tuple(SIZES)
BLOCK = 192
PART = 96
HALF = 48
HD = 128
EXTRA = 16
OFFSETS = (0, -1, 1, 2)
LOW = -1e30
MASKED = -2e30
RATE = math.log2(math.e) / math.sqrt(HD)


def permute(array, axes, move):
    axes = [a for a in AXES if a in axes]

    def index(at):
        return functools.reduce(lambda n, a: n * SIZES[a] + at[a] % SIZES[a], axes, 0)

    pairs = []
    for spot in itertools.product(*[range(SIZES[a]) for a in axes]):
        at = dict(zip(axes, spot))
        pairs.append((index(at), index({**at, **move(at)})))
    return lax.ppermute(array, tuple(axes), pairs)


def ring(array, first, step):
    second = "y" if first == "x" else "x"

    def move(at):
        axis = first if at["core"] == 0 else second
        return {axis: at[axis] + step}

    return permute(array, ("core", "y", "x"), move)


def attention_kernel(plan, *refs):
    q_refs, kv_refs = refs[0:4], refs[4:8]
    out_refs = refs[8:12]
    q_all, k_all, v_all, top, total, acc = refs[12:]
    swap = plan[0]

    def place(row):
        odd = lax.rem(row // HALF, 2)
        return row + swap * HALF * (1 - 2 * odd)

    for s in range(4):
        for z in range(8):
            i, at = z // 2, (z % 2) * PART
            q_all[i, s * BLOCK + at : s * BLOCK + at + PART, :] = q_refs[s][z, 0:PART, :]
            k_all[4 * s + i, at : at + PART, :] = kv_refs[s][z, EXTRA : EXTRA + PART, :]
            v_all[4 * s + i, at : at + PART, :] = kv_refs[s][z, EXTRA + PART :, :]

    lane = lax.broadcasted_iota(jnp.int32, (1, 4 * BLOCK), 1)
    lane_slot = lane // BLOCK
    lane_place = place(lane - lane_slot * BLOCK)
    row_place = place(lax.broadcasted_iota(jnp.int32, (BLOCK, 1), 0))

    for i in range(4):
        top[...] = jnp.full_like(top, LOW)
        total[...] = jnp.zeros_like(total)
        acc[...] = jnp.zeros_like(acc)
        queries = q_all.at[i]

        def update(kb, masked):
            scores = lax.dot_general(
                k_all[kb], queries[...], (((1,), (1,)), ((), ())), preferred_element_type=jnp.float32
            )
            if masked:
                q_doc = jnp.zeros_like(lane)
                q_base = jnp.zeros_like(lane)
                for s in range(4):
                    doc = jnp.zeros_like(lane)
                    for d in range(1, 8):
                        doc += (plan[80 + 32 * s + 8 * i + d] <= lane_place).astype(jnp.int32)
                    q_doc = jnp.where(lane_slot == s, doc, q_doc)
                    q_base = jnp.where(lane_slot == s, plan[1 + s] + 16 * i, q_base)
                k_doc = jnp.zeros_like(row_place)
                for d in range(1, 8):
                    k_doc += (plan[208 + 8 * kb + d] <= row_place).astype(jnp.int32)
                k_base = plan[5 + kb // 4] + 16 * lax.rem(kb, 4)
                q_pos = q_base * BLOCK + lane_place
                k_pos = k_base * BLOCK + row_place
                scores = jnp.where((k_doc == q_doc) & (k_pos <= q_pos), scores, MASKED)
            old = top[...]
            new = jnp.maximum(old, jnp.max(scores, axis=0, keepdims=True))
            weights = jnp.exp2((scores - new) * RATE)
            keep = jnp.exp2((old - new) * RATE)
            top[...] = new
            total[...] = total[...] * keep + jnp.sum(weights, axis=0, keepdims=True)
            acc[...] = acc[...] * keep + lax.dot_general(
                v_all[kb], weights.astype(jnp.bfloat16), (((0,), (0,)), ((), ())), preferred_element_type=jnp.float32
            )

        def visit(n, carry):
            kb = (n // (i + 1)) * 4 + lax.rem(n, i + 1)
            code = plan[16 + 16 * i + kb]

            @pl.when(code == 1)
            def _():
                update(kb, False)

            @pl.when(code == 2)
            def _():
                update(kb, True)

            return carry

        lax.fori_loop(0, 4 * (i + 1), visit, 0)
        some = total[...] > 0
        scale = jnp.where(some, 1.0 / jnp.where(some, total[...], 1.0), 0.0)
        level = jnp.where(some, top[...] * RATE + jnp.log2(jnp.where(some, total[...], 1.0)), LOW)
        result = (acc[...] * scale).astype(jnp.bfloat16)
        high = level.astype(jnp.bfloat16)
        rest = level - high.astype(jnp.float32)
        middle = rest.astype(jnp.bfloat16)
        low = (rest - middle.astype(jnp.float32)).astype(jnp.bfloat16)
        digits = jnp.concatenate(
            [jnp.broadcast_to(part, (8, 4 * BLOCK)) for part in (high, middle, low, low)], axis=0
        )
        for s in range(4):
            lanes, to = slice(s * BLOCK, (s + 1) * BLOCK), slice(i * BLOCK, (i + 1) * BLOCK)
            out_refs[s][0:HD, to] = result[:, lanes]
            out_refs[s][HD:, to] = digits[:, lanes]


def combine_kernel(where, *refs):
    parts, out_ref, held = refs[0:4], refs[4], refs[5]
    levels = []
    for part in parts:
        digits = part[HD:, :].astype(jnp.float32)
        levels.append(digits[0:1] + digits[8:9] + digits[16:17])
    peak = functools.reduce(jnp.maximum, levels)
    shares = [jnp.exp2(level - peak) for level in levels]
    whole = functools.reduce(jnp.add, shares)
    summed = jnp.zeros((HD, 4 * BLOCK), jnp.float32)
    for part, share in zip(parts, shares):
        summed += part[0:HD, :].astype(jnp.float32) * (share / whole)
    held[...] = summed.T.astype(jnp.bfloat16)
    zl, core = where[0], where[1]
    side = 1 - 2 * core
    for zh in range(4):
        z = 2 * zh + zl
        keep = lax.rem(z + side + 8, 8)
        give = lax.rem(z - side + 8, 8)
        for n, row in enumerate((z * PART, keep * PART, z * PART + HALF, give * PART + HALF)):
            row = pl.multiple_of(row, EXTRA)
            out_ref[zh, n * HALF : (n + 1) * HALF, :] = held[pl.ds(row, HALF), :]


def vmem(n):
    return [pl.BlockSpec(memory_space=pltpu.VMEM)] * n


def attend(plan, queries, keys_values):
    piece = jax.ShapeDtypeStruct((HD + 32, 4 * BLOCK), jnp.bfloat16)
    return pl.pallas_call(
        attention_kernel,
        out_shape=[piece] * 4,
        in_specs=[pl.BlockSpec(memory_space=pltpu.SMEM)] + vmem(8),
        out_specs=vmem(4),
        scratch_shapes=[
            pltpu.VMEM((4, 4 * BLOCK, HD), jnp.bfloat16),
            pltpu.VMEM((16, BLOCK, HD), jnp.bfloat16),
            pltpu.VMEM((16, BLOCK, HD), jnp.bfloat16),
            pltpu.VMEM((1, 4 * BLOCK), jnp.float32),
            pltpu.VMEM((1, 4 * BLOCK), jnp.float32),
            pltpu.VMEM((HD, 4 * BLOCK), jnp.float32),
        ],
        compiler_params=pltpu.CompilerParams(vmem_limit_bytes=40 * 1024 * 1024),
    )(plan, *queries, *keys_values)


def combine(where, pieces):
    return pl.pallas_call(
        combine_kernel,
        out_shape=jax.ShapeDtypeStruct((4, BLOCK, HD), jnp.bfloat16),
        in_specs=[pl.BlockSpec(memory_space=pltpu.SMEM)] + vmem(4),
        out_specs=vmem(1)[0],
        scratch_shapes=[pltpu.VMEM((4 * BLOCK, HD), jnp.bfloat16)],
        compiler_params=pltpu.CompilerParams(vmem_limit_bytes=40 * 1024 * 1024),
    )(where, *pieces)


def make_plan(core, y, x, queries, keys_values):
    def counts(arrays, row):
        return jnp.stack([a[::2, row, :8] for a in arrays]).astype(jnp.int32)

    offsets = jnp.array(OFFSETS, jnp.int32)
    along_x = 4 * y + (x + offsets) % 4
    along_y = 4 * ((y + offsets) % 4) + x
    q_base = jnp.where(core == 0, along_x, along_y)
    k_base = jnp.where(core == 0, along_y, along_x)
    q_counts, k_counts = counts(queries, PART), counts(keys_values, 0)

    def first(c):
        return jnp.sum((c[..., 1:] == 0).astype(jnp.int32), axis=-1)

    def last(c):
        return jnp.sum((c[..., 1:] < BLOCK).astype(jnp.int32), axis=-1)

    step = 16 * jnp.arange(4, dtype=jnp.int32)
    q_at = (q_base[:, None] + step)[:, :, None, None]
    k_at = (k_base[:, None] + step)[None, None]
    q_first, q_last = first(q_counts)[:, :, None, None], last(q_counts)[:, :, None, None]
    k_first, k_last = first(k_counts)[None, None], last(k_counts)[None, None]
    some = jnp.any((q_at >= k_at) & (k_last >= q_first), axis=0)
    full = jnp.all((q_at > k_at) & (k_first == q_last), axis=0)
    code = jnp.where(full, 1, jnp.where(some, 2, 0)).astype(jnp.int32)
    head = jnp.concatenate([core[None], q_base, k_base, jnp.zeros((7,), jnp.int32)])
    return jnp.concatenate([head, code.reshape(-1), q_counts.reshape(-1), k_counts.reshape(-1)])


def body(query, key_in, value, doc_ids, out_weight):
    zl, core, zh, y, x = [lax.axis_index(a).astype(jnp.int32) for a in AXES]

    def heads_of(array, c):
        array = array.reshape(HALF, 2, 2, 4, HD)
        array = lax.dynamic_index_in_dim(array, c, 2, keepdims=False)
        return array.transpose(2, 1, 0, 3).reshape(8, HALF, HD)

    mine = [heads_of(a, core) for a in (query, key_in, value)]
    theirs = jnp.stack([heads_of(a, 1 - core) for a in (query, key_in, value)], axis=1)
    theirs = permute(theirs, ("core",), lambda at: {"core": at["core"] + 1})
    marks = jnp.arange(8, dtype=jnp.int32)
    counts = jnp.sum((doc_ids[None, :] < marks[:, None]).astype(jnp.float32), axis=1).astype(jnp.bfloat16)
    extra = jnp.broadcast_to(jnp.pad(counts, (0, HD - 8)), (8, EXTRA, HD))
    sent = jnp.concatenate(
        [mine[0], theirs[:, 0], extra, mine[1], theirs[:, 1], mine[2], theirs[:, 2]], axis=1
    )
    held = lax.all_to_all(sent, ("zh", "zl"), 0, 0, tiled=True)
    own_q, own_kv = held[:, : PART + EXTRA], held[:, PART:]
    queries = [own_q] + [ring(own_q, "x", -step) for step in OFFSETS[1:]]
    keys_values = [own_kv] + [ring(own_kv, "y", -step) for step in OFFSETS[1:]]
    plan = make_plan(core, y, x, queries, keys_values)
    pieces = attend(plan, queries, keys_values)
    pieces = [pieces[0]] + [ring(p, "x", step) for p, step in zip(pieces[1:], OFFSETS[1:])]
    attended = combine(jnp.stack([zl, core]), pieces)
    attended = lax.all_to_all(attended, "zh", 0, 0, tiled=True)
    attended = attended.transpose(1, 0, 2).reshape(BLOCK, 4 * HD)
    mixed = jnp.dot(attended, out_weight, preferred_element_type=jnp.float32).astype(jnp.bfloat16)
    other = permute(mixed[PART:], ("core",), lambda at: {"core": at["core"] + 1})
    chip = mixed[:PART].astype(jnp.float32) + other.astype(jnp.float32)

    def next_chip(at):
        z = (2 * at["zh"] + at["zl"] + (1 if at["core"] == 0 else -1)) % 8
        return {"zh": z // 2, "zl": z % 2}

    beside = permute(chip[HALF:].astype(jnp.bfloat16), ("zl", "core", "zh"), next_chip)
    return (chip[:HALF] + beside.astype(jnp.float32)).astype(jnp.bfloat16)[None]


def solution(mesh):
    apart = Mesh(mesh.devices.reshape(tuple(SIZES.values())), AXES)
    block, head = ("zh", "y", "x"), ("zl", "core")
    array = P(block, head, None, None)
    return jax.shard_map(
        body,
        mesh=apart,
        in_specs=(array, array, array, P(block), P(head, None)),
        out_specs=P(block, head, None),
        check_vma=False,
    )
```

```python
import functools
import itertools
import math

import jax
import jax.numpy as jnp
from jax import lax
from jax.experimental import pallas as pl
from jax.experimental.pallas import tpu as pltpu
from jax.sharding import Mesh
from jax.sharding import PartitionSpec as P

SIZES = {"zl": 2, "core": 2, "zh": 4, "y": 4, "x": 4}
AXES = tuple(SIZES)
BLOCK = 192
PART = 96
HALF = 48
HD = 128
EXTRA = 16
OFFSETS = (0, 1, 2, -1)
LOW = -1e30
MASKED = -2e30
SPAN = 1 << 14
WIDE = 2 * BLOCK
GROUPS = 8
SPARE = 16
RATE = math.log2(math.e) / math.sqrt(HD)


def permute(array, axes, move):
    axes = [a for a in AXES if a in axes]

    def index(at):
        return functools.reduce(lambda n, a: n * SIZES[a] + at[a] % SIZES[a], axes, 0)

    pairs = []
    for spot in itertools.product(*[range(SIZES[a]) for a in axes]):
        at = dict(zip(axes, spot))
        pairs.append((index(at), index({**at, **move(at)})))
    return lax.ppermute(array, tuple(axes), pairs)


def ring(array, first, step):
    second = "y" if first == "x" else "x"

    def move(at):
        axis = first if at["core"] == 0 else second
        return {axis: at[axis] + step}

    return permute(array, ("core", "y", "x"), move)


def at_spot():
    return [lax.axis_index(a).astype(jnp.int32) for a in AXES]


def attention_kernel(*refs):
    q_refs, kv_refs, out_ref = refs[0:4], refs[4:8], refs[8]
    q_all, k_all, v_all, k_code, q_code, top, total, acc = refs[9:17]
    scores_of, weights_of, keep_of, peak_of = refs[17:19], refs[19:21], refs[21:23], refs[23:25]
    tile_keys, tile_group, table, plan, sent = refs[25:30]
    _, swap, _, y, x = at_spot()
    mine = jnp.where(swap == 0, x, y)
    theirs = jnp.where(swap == 0, y, x)

    def place(row):
        odd = lax.rem(row // HALF, 2)
        return row + swap * HALF * (1 - 2 * odd)

    def slot_of(at):
        return lax.rem(at - mine + 4, 4)

    def q_base(at):
        return jnp.where(swap == 0, 4 * y + at, 4 * at + x)

    def k_base(at):
        return jnp.where(swap == 0, 4 * at + x, 4 * y + at)

    for s in range(4):
        for i in range(4):
            n = 4 * s + i
            q_row = q_refs[s][2 * i, PART : PART + EXTRA, :].astype(jnp.float32)
            k_row = kv_refs[s][2 * i, 0:EXTRA, :].astype(jnp.float32)
            table[n : n + 1, :] = q_row[0:1].astype(jnp.int32)
            table[16 + n : 17 + n, :] = k_row[0:1].astype(jnp.int32)
    counts = table[...]
    row = lax.broadcasted_iota(jnp.int32, counts.shape, 0)
    lane = lax.broadcasted_iota(jnp.int32, counts.shape, 1)

    def tally(mask, axis):
        return jnp.sum(jnp.where(mask, 1.0, 0.0), axis=axis, keepdims=True)

    inner = (lane >= 1) & (lane < 8)
    first, last = tally(inner & (counts == 0), 1), tally(inner & (counts < BLOCK), 1)
    k_last = jnp.sum(jnp.where(row == lane + 16, last, 0.0), axis=0, keepdims=True)
    q_at = q_base(lax.rem(mine + row // 4, 4)) + 16 * lax.rem(row, 4)
    k_at = k_base(lax.rem(theirs + lane // 4, 4)) + 16 * lax.rem(lane, 4)
    some = (q_at >= k_at) & (k_last >= first) & (lane < 16)
    bits = jnp.sum(jnp.where(some, lax.shift_left(1, jnp.minimum(lane, 16)).astype(jnp.float32), 0.0), axis=1, keepdims=True)
    for at, column in ((8, first), (9, last), (10, bits)):
        counts = jnp.where(lane == at, column.astype(jnp.int32), counts)
    table[...] = counts
    copy = pltpu.make_async_copy(table, plan, sent)
    copy.start()

    for s in range(4):
        at = lax.rem(mine + s, 4) * BLOCK
        for z in range(8):
            i, row = z // 2, (z % 2) * PART
            to = pl.multiple_of(at + row, PART)
            q_all[i, pl.ds(to, PART), :] = q_refs[s][z, 0:PART, :]
            k_all[4 * s + i, row : row + PART, :] = kv_refs[s][z, EXTRA : EXTRA + PART, :]
            v_all[4 * s + i, row : row + PART, :] = kv_refs[s][z, EXTRA + PART :, :]
    k_all[SPARE] = jnp.zeros((BLOCK, HD), jnp.bfloat16)
    v_all[SPARE] = jnp.zeros((BLOCK, HD), jnp.bfloat16)
    top[...] = jnp.full_like(top, LOW)
    total[...] = jnp.zeros_like(total)
    acc[...] = jnp.zeros_like(acc)
    copy.wait()

    def clear(n):
        tile_keys[2 * n] = SPARE
        tile_keys[2 * n + 1] = SPARE
        tile_group[n] = GROUPS

    clear(0)
    clear(1)
    end = jnp.int32(4)
    for group in range(GROUPS):
        i, first = group // 2, 2 * (group % 2)
        bits = plan[4 * slot_of(first) + i, 10] | plan[4 * slot_of(first + 1) + i, 10]
        for slot in range(4):
            for j in range(i + 1):
                kb = 4 * slot + j
                tile_keys[end] = kb
                tile_group[end // 2] = group
                end = end + (lax.shift_right_logical(bits, kb) & 1)
        tile_keys[end] = SPARE
        end = ((end + 1) // 2) * 2
    tiles = end // 2
    for n in range(4):
        clear(tiles + n)

    row_place = place(lax.broadcasted_iota(jnp.int32, (BLOCK, HD), 0))
    for kb in range(16):
        base = (k_base(lax.rem(theirs + kb // 4, 4)) + 16 * (kb % 4)) * BLOCK
        first, last = plan[16 + kb, 8], plan[16 + kb, 9]
        k_code[kb] = (row_place + (base + first * SPAN)).astype(jnp.uint32)

        def add(d, carry, kb=kb):
            k_code[kb] += jnp.where(plan[16 + kb, d] <= row_place, SPAN, 0).astype(jnp.uint32)
            return carry

        lax.fori_loop(first + 1, last + 1, add, 0)
    k_code[SPARE] = jnp.full((BLOCK, HD), 1 << 30, jnp.uint32)
    lane = lax.broadcasted_iota(jnp.int32, (1, WIDE), 1)
    second = lane >= BLOCK
    lane_place = place(jnp.where(second, lane - BLOCK, lane))
    for group in range(GROUPS):
        i, first = group // 2, 2 * (group % 2)
        slots = [slot_of(first), slot_of(first + 1)]
        code = lane_place + jnp.where(second, q_base(first + 1), q_base(first)) * BLOCK + 16 * i * BLOCK
        for d in range(1, 8):
            counts = [plan[4 * slot + i, d] for slot in slots]
            code += jnp.where(jnp.where(second, counts[1], counts[0]) <= lane_place, SPAN, 0)
        q_code[group] = code.astype(jnp.uint32)
    q_code[GROUPS] = jnp.zeros((1, WIDE), jnp.uint32)

    def stage(n, odd):
        group = tile_group[n + 2]
        row = pl.multiple_of(lax.rem(group, 2) * WIDE, WIDE)
        queries = q_all[group // 2, pl.ds(row, WIDE), :]
        q_row = q_code[group]
        peaks = []
        for half in range(2):
            kb = tile_keys[2 * n + 4 + half]
            scores = lax.dot_general(
                k_all[kb], queries, (((1,), (1,)), ((), ())), preferred_element_type=jnp.float32
            )
            ahead = q_row - jnp.concatenate([k_code[kb]] * (WIDE // HD), axis=1)
            scores = jnp.where(ahead < SPAN, scores, MASKED)
            scores_of[odd][half * BLOCK : (half + 1) * BLOCK, :] = scores
            peaks.append(jnp.max(scores, axis=0, keepdims=True))
        peak_of[odd][...] = jnp.maximum(peaks[0], peaks[1])

        group = tile_group[n + 1]
        old = top[group]
        new = jnp.maximum(old, peak_of[1 - odd][...])
        keep = jnp.exp2((old - new) * RATE)
        top[group] = new
        keep_of[1 - odd][...] = keep
        weights = jnp.exp2((scores_of[1 - odd][...] - new) * RATE)
        total[group] = total[group] * keep + jnp.sum(weights, axis=0, keepdims=True)
        weights_of[1 - odd][...] = weights.astype(jnp.bfloat16)

        group = tile_group[n]
        product = acc[group] * keep_of[odd][...]
        for half in range(2):
            product += lax.dot_general(
                v_all[tile_keys[2 * n + half]],
                weights_of[odd][half * BLOCK : (half + 1) * BLOCK, :],
                (((0,), (0,)), ((), ())),
                preferred_element_type=jnp.float32,
            )
        acc[group] = product

    def step(n, carry):
        stage(2 * n, 0)
        stage(2 * n + 1, 1)
        return carry

    lax.fori_loop(0, (tiles + 1) // 2, step, 0)

    for group in range(GROUPS):
        i, first = group // 2, 2 * (group % 2)
        some = total[group] > 0
        whole = jnp.where(some, total[group], 1.0)
        level = jnp.where(some, top[group] * RATE + jnp.log2(whole), LOW)
        result = (acc[group] * jnp.where(some, 1.0 / whole, 0.0)).astype(jnp.bfloat16)
        high = level.astype(jnp.bfloat16)
        rest = level - high.astype(jnp.float32)
        middle = rest.astype(jnp.bfloat16)
        low = rest - middle.astype(jnp.float32)
        row = lax.broadcasted_iota(jnp.int32, (EXTRA, WIDE), 0)
        digits = jnp.where(row == 0, high.astype(jnp.float32), jnp.where(row == 1, middle.astype(jnp.float32), low))
        digits = digits.astype(jnp.bfloat16)
        for half in range(2):
            slot = slot_of(first + half)
            lanes, to = slice(half * BLOCK, (half + 1) * BLOCK), slice(i * BLOCK, (i + 1) * BLOCK)
            out_ref[slot, 0:HD, to] = result[:, lanes]
            out_ref[slot, HD:, to] = digits[:, lanes]


def combine_kernel(*refs):
    parts, out_ref = refs[0:4], refs[4]
    levels = []
    for part in parts:
        digits = part[HD:, :].astype(jnp.float32)
        levels.append(digits[0:1] + digits[1:2] + digits[2:3])
    peak = functools.reduce(jnp.maximum, levels)
    shares = [jnp.exp2(level - peak) for level in levels]
    whole = functools.reduce(jnp.add, shares)
    summed = jnp.zeros((HD, 4 * BLOCK), jnp.float32)
    for part, share in zip(parts, shares):
        summed += part[0:HD, :].astype(jnp.float32) * (share / whole)
    out_ref[...] = summed.T.astype(jnp.bfloat16)


def project_kernel(heads_ref, own_ref, beside_ref, out_ref, held):
    zl, tile = at_spot()[0], 1024
    for zh in range(4):
        columns = slice(zh * HD, (zh + 1) * HD)
        held[0, :, columns] = heads_ref[2 * zh + zl]
        held[1, :, columns] = heads_ref[2 * zh + 1 - zl]

    def step(n, carry):
        columns = pl.ds(pl.multiple_of(n * tile, tile), tile)
        product = jnp.dot(held[0], own_ref[:, columns], preferred_element_type=jnp.float32)
        product += jnp.dot(held[1], beside_ref[:, columns], preferred_element_type=jnp.float32)
        out_ref[:, columns] = product.astype(jnp.bfloat16)
        return carry

    lax.fori_loop(0, out_ref.shape[1] // tile, step, 0)


def vmem(n):
    return [pl.BlockSpec(memory_space=pltpu.VMEM)] * n


def attend(queries, keys_values):
    block = (SPARE + 1, BLOCK, HD)
    row = (GROUPS + 1, 1, WIDE)
    return pl.pallas_call(
        attention_kernel,
        out_shape=jax.ShapeDtypeStruct((4, HD + EXTRA, 4 * BLOCK), jnp.bfloat16),
        in_specs=vmem(8),
        out_specs=vmem(1)[0],
        scratch_shapes=[
            pltpu.VMEM((GROUPS // 2 + 1, 4 * BLOCK, HD), jnp.bfloat16),
            pltpu.VMEM(block, jnp.bfloat16),
            pltpu.VMEM(block, jnp.bfloat16),
            pltpu.VMEM(block, jnp.uint32),
            pltpu.VMEM(row, jnp.uint32),
            pltpu.VMEM(row, jnp.float32),
            pltpu.VMEM(row, jnp.float32),
            pltpu.VMEM((GROUPS + 1, HD, WIDE), jnp.float32),
            pltpu.VMEM((WIDE, WIDE), jnp.float32),
            pltpu.VMEM((WIDE, WIDE), jnp.float32),
            pltpu.VMEM((WIDE, WIDE), jnp.bfloat16),
            pltpu.VMEM((WIDE, WIDE), jnp.bfloat16),
            pltpu.VMEM((1, WIDE), jnp.float32),
            pltpu.VMEM((1, WIDE), jnp.float32),
            pltpu.VMEM((1, WIDE), jnp.float32),
            pltpu.VMEM((1, WIDE), jnp.float32),
            pltpu.SMEM((192,), jnp.int32),
            pltpu.SMEM((96,), jnp.int32),
            pltpu.VMEM((32, HD), jnp.int32),
            pltpu.SMEM((32, HD), jnp.int32),
            pltpu.SemaphoreType.DMA,
        ],
        compiler_params=pltpu.CompilerParams(vmem_limit_bytes=10 * 1024 * 1024),
    )(*queries, *keys_values)


def combine(pieces):
    return pl.pallas_call(
        combine_kernel,
        out_shape=jax.ShapeDtypeStruct((4 * BLOCK, HD), jnp.bfloat16),
        in_specs=vmem(4),
        out_specs=vmem(1)[0],
        compiler_params=pltpu.CompilerParams(vmem_limit_bytes=8 * 1024 * 1024),
    )(*pieces)


def project(heads, own, beside):
    return pl.pallas_call(
        project_kernel,
        out_shape=jax.ShapeDtypeStruct((PART, own.shape[1]), jnp.bfloat16),
        in_specs=vmem(3),
        out_specs=vmem(1)[0],
        scratch_shapes=[pltpu.VMEM((2, PART, 4 * HD), jnp.bfloat16)],
        compiler_params=pltpu.CompilerParams(vmem_limit_bytes=10 * 1024 * 1024),
    )(heads, own, beside)


def body(query, key_in, value, doc_ids, out_weight):
    core = lax.axis_index("core").astype(jnp.int32)

    def heads_of(array, c):
        array = array.reshape(HALF, 2, 2, 4, HD)
        array = lax.dynamic_index_in_dim(array, c, 2, keepdims=False)
        return array.transpose(2, 1, 0, 3).reshape(8, HALF, HD)

    mine = [heads_of(a, core) for a in (query, key_in, value)]
    theirs = jnp.stack([heads_of(a, 1 - core) for a in (query, key_in, value)], axis=1)
    theirs = permute(theirs, ("core",), lambda at: {"core": at["core"] + 1})
    marks = jnp.arange(8, dtype=jnp.int32)
    counts = jnp.sum((doc_ids[None, :] < marks[:, None]).astype(jnp.float32), axis=1).astype(jnp.bfloat16)
    extra = jnp.broadcast_to(jnp.pad(counts, (0, HD - 8)), (8, EXTRA, HD))
    sent = jnp.concatenate(
        [mine[0], theirs[:, 0], extra, mine[1], theirs[:, 1], mine[2], theirs[:, 2]], axis=1
    )
    held = lax.all_to_all(sent, ("zh", "zl"), 0, 0, tiled=True)
    held, weight = lax.optimization_barrier((held, out_weight))

    def next_chip(at):
        z = (2 * at["zh"] + at["zl"] + (1 if at["core"] == 0 else -1)) % 8
        return {"zh": z // 2, "zl": z % 2}

    beside = permute(weight, ("zl", "core", "zh"), next_chip)
    own_q, own_kv = held[:, : PART + EXTRA], held[:, PART:]
    after, before = ring(own_kv, "y", -1), ring(own_kv, "y", 1)
    keys_values = [own_kv, after, ring(after, "y", -1), before]
    q_before = ring(own_q, "x", 1)
    queries = [own_q, ring(own_q, "x", -1), ring(q_before, "x", 1), q_before]
    pieces = attend(queries, keys_values)
    pieces = [pieces[0]] + [ring(pieces[s], "x", OFFSETS[s]) for s in (1, 3, 2)]
    attended = combine(pieces).reshape(8, PART, HD)
    heads = lax.all_to_all(attended, ("zh", "zl"), 0, 0, tiled=True)
    mixed = project(heads, out_weight, beside)
    other = permute(mixed[HALF:], ("core",), lambda at: {"core": at["core"] + 1})
    return (mixed[:HALF].astype(jnp.float32) + other.astype(jnp.float32)).astype(jnp.bfloat16)[None]


def solution(mesh):
    apart = Mesh(mesh.devices.reshape(tuple(SIZES.values())), AXES)
    block, head = ("zh", "y", "x"), ("zl", "core")
    array = P(block, head, None, None)
    return jax.shard_map(
        body,
        mesh=apart,
        in_specs=(array, array, array, P(block), P(head, None)),
        out_specs=P(block, head, None),
        check_vma=False,
    )
```

```python
import functools
import itertools
import math

import jax
import jax.numpy as jnp
from jax import lax
from jax.experimental import pallas as pl
from jax.experimental.pallas import tpu as pltpu
from jax.sharding import Mesh
from jax.sharding import PartitionSpec as P

SIZES = {"zl": 2, "core": 2, "zh": 4, "y": 4, "x": 4}
AXES = tuple(SIZES)
BLOCK = 192
PART = 96
HALF = 48
HD = 128
EXTRA = 16
OFFSETS = (0, 1, 2, -1)
LOW = -1e30
MASKED = -2e30
SPAN = 1 << 14
WIDE = 2 * BLOCK
GROUPS = 8
SPARE = 16
RATE = math.log2(math.e) / math.sqrt(HD)


def permute(array, axes, move):
    axes = [a for a in AXES if a in axes]

    def index(at):
        return functools.reduce(lambda n, a: n * SIZES[a] + at[a] % SIZES[a], axes, 0)

    pairs = []
    for spot in itertools.product(*[range(SIZES[a]) for a in axes]):
        at = dict(zip(axes, spot))
        pairs.append((index(at), index({**at, **move(at)})))
    return lax.ppermute(array, tuple(axes), pairs)


def ring(array, first, step):
    second = "y" if first == "x" else "x"

    def move(at):
        axis = first if at["core"] == 0 else second
        return {axis: at[axis] + step}

    return permute(array, ("core", "y", "x"), move)


def at_spot():
    return [lax.axis_index(a).astype(jnp.int32) for a in AXES]


def attention_kernel(*refs):
    q_refs, kv_refs, out_ref = refs[0:4], refs[4:8], refs[8]
    q_all, k_all, v_all, k_code, q_code, top, total, acc = refs[9:17]
    scores_of, weights_of, keep_of, peak_of = refs[17:19], refs[19:21], refs[21:23], refs[23:25]
    tile_keys, tile_group, table, plan, sent = refs[25:30]
    _, swap, _, y, x = at_spot()
    mine = jnp.where(swap == 0, x, y)
    theirs = jnp.where(swap == 0, y, x)

    def place(row):
        odd = lax.rem(row // HALF, 2)
        return row + swap * HALF * (1 - 2 * odd)

    def slot_of(at):
        return lax.rem(at - mine + 4, 4)

    def q_base(at):
        return jnp.where(swap == 0, 4 * y + at, 4 * at + x)

    def k_base(at):
        return jnp.where(swap == 0, 4 * at + x, 4 * y + at)

    for s in range(4):
        for i in range(4):
            n = 4 * s + i
            q_row = q_refs[s][2 * i, PART : PART + EXTRA, :].astype(jnp.float32)
            k_row = kv_refs[s][2 * i, 0:EXTRA, :].astype(jnp.float32)
            table[n : n + 1, :] = q_row[0:1].astype(jnp.int32)
            table[16 + n : 17 + n, :] = k_row[0:1].astype(jnp.int32)
    counts = table[...]
    row = lax.broadcasted_iota(jnp.int32, counts.shape, 0)
    lane = lax.broadcasted_iota(jnp.int32, counts.shape, 1)

    def tally(mask, axis):
        return jnp.sum(jnp.where(mask, 1.0, 0.0), axis=axis, keepdims=True)

    inner = (lane >= 1) & (lane < 8)
    first, last = tally(inner & (counts == 0), 1), tally(inner & (counts < BLOCK), 1)
    k_last = jnp.sum(jnp.where(row == lane + 16, last, 0.0), axis=0, keepdims=True)
    q_at = q_base(lax.rem(mine + row // 4, 4)) + 16 * lax.rem(row, 4)
    k_at = k_base(lax.rem(theirs + lane // 4, 4)) + 16 * lax.rem(lane, 4)
    some = (q_at >= k_at) & (k_last >= first) & (lane < 16)
    bits = jnp.sum(jnp.where(some, lax.shift_left(1, jnp.minimum(lane, 16)).astype(jnp.float32), 0.0), axis=1, keepdims=True)
    for at, column in ((8, first), (9, last), (10, bits)):
        counts = jnp.where(lane == at, column.astype(jnp.int32), counts)
    table[...] = counts
    copy = pltpu.make_async_copy(table, plan, sent)
    copy.start()

    for s in range(4):
        at = lax.rem(mine + s, 4) * BLOCK
        for z in range(8):
            i, row = z // 2, (z % 2) * PART
            to = pl.multiple_of(at + row, PART)
            q_all[i, pl.ds(to, PART), :] = q_refs[s][z, 0:PART, :]
            k_all[4 * s + i, row : row + PART, :] = kv_refs[s][z, EXTRA : EXTRA + PART, :]
            v_all[4 * s + i, row : row + PART, :] = kv_refs[s][z, EXTRA + PART :, :]
    k_all[SPARE] = jnp.zeros((BLOCK, HD), jnp.bfloat16)
    v_all[SPARE] = jnp.zeros((BLOCK, HD), jnp.bfloat16)
    top[...] = jnp.full_like(top, LOW)
    total[...] = jnp.zeros_like(total)
    acc[...] = jnp.zeros_like(acc)
    copy.wait()

    def clear(n):
        tile_keys[2 * n] = SPARE
        tile_keys[2 * n + 1] = SPARE
        tile_group[n] = GROUPS

    clear(0)
    clear(1)
    end = jnp.int32(4)
    for group in range(GROUPS):
        i, first = group // 2, 2 * (group % 2)
        bits = plan[4 * slot_of(first) + i, 10] | plan[4 * slot_of(first + 1) + i, 10]
        for slot in range(4):
            for j in range(i + 1):
                kb = 4 * slot + j
                tile_keys[end] = kb
                tile_group[end // 2] = group
                end = end + (lax.shift_right_logical(bits, kb) & 1)
        tile_keys[end] = SPARE
        end = ((end + 1) // 2) * 2
    tiles = end // 2
    for n in range(4):
        clear(tiles + n)

    row_place = place(lax.broadcasted_iota(jnp.int32, (BLOCK, HD), 0))
    for kb in range(16):
        base = (k_base(lax.rem(theirs + kb // 4, 4)) + 16 * (kb % 4)) * BLOCK
        first, last = plan[16 + kb, 8], plan[16 + kb, 9]
        k_code[kb] = (row_place + (base + first * SPAN)).astype(jnp.uint32)

        def add(d, carry, kb=kb):
            k_code[kb] += jnp.where(plan[16 + kb, d] <= row_place, SPAN, 0).astype(jnp.uint32)
            return carry

        lax.fori_loop(first + 1, last + 1, add, 0)
    k_code[SPARE] = jnp.full((BLOCK, HD), 1 << 30, jnp.uint32)
    lane = lax.broadcasted_iota(jnp.int32, (1, WIDE), 1)
    second = lane >= BLOCK
    lane_place = place(jnp.where(second, lane - BLOCK, lane))
    for group in range(GROUPS):
        i, first = group // 2, 2 * (group % 2)
        slots = [slot_of(first), slot_of(first + 1)]
        code = lane_place + jnp.where(second, q_base(first + 1), q_base(first)) * BLOCK + 16 * i * BLOCK
        for d in range(1, 8):
            counts = [plan[4 * slot + i, d] for slot in slots]
            code += jnp.where(jnp.where(second, counts[1], counts[0]) <= lane_place, SPAN, 0)
        q_code[group] = code.astype(jnp.uint32)
    q_code[GROUPS] = jnp.zeros((1, WIDE), jnp.uint32)

    def stage(n, odd):
        group = tile_group[n + 2]
        row = pl.multiple_of(lax.rem(group, 2) * WIDE, WIDE)
        queries = q_all[group // 2, pl.ds(row, WIDE), :]
        q_row = q_code[group]
        peaks = []
        for half in range(2):
            kb = tile_keys[2 * n + 4 + half]
            scores = lax.dot_general(
                k_all[kb], queries, (((1,), (1,)), ((), ())), preferred_element_type=jnp.float32
            )
            ahead = q_row - jnp.concatenate([k_code[kb]] * (WIDE // HD), axis=1)
            scores = jnp.where(ahead < SPAN, scores, MASKED)
            scores_of[odd][half * BLOCK : (half + 1) * BLOCK, :] = scores
            peaks.append(jnp.max(scores, axis=0, keepdims=True))
        peak_of[odd][...] = jnp.maximum(peaks[0], peaks[1])

        group = tile_group[n + 1]
        old = top[group]
        new = jnp.maximum(old, peak_of[1 - odd][...])
        keep = jnp.exp2((old - new) * RATE)
        top[group] = new
        keep_of[1 - odd][...] = keep
        weights = jnp.exp2((scores_of[1 - odd][...] - new) * RATE)
        total[group] = total[group] * keep + jnp.sum(weights, axis=0, keepdims=True)
        weights_of[1 - odd][...] = weights.astype(jnp.bfloat16)

        group = tile_group[n]
        product = acc[group] * keep_of[odd][...]
        for half in range(2):
            product += lax.dot_general(
                v_all[tile_keys[2 * n + half]],
                weights_of[odd][half * BLOCK : (half + 1) * BLOCK, :],
                (((0,), (0,)), ((), ())),
                preferred_element_type=jnp.float32,
            )
        acc[group] = product

    def step(n, carry):
        stage(2 * n, 0)
        stage(2 * n + 1, 1)
        return carry

    lax.fori_loop(0, (tiles + 1) // 2, step, 0)

    for group in range(GROUPS):
        i, first = group // 2, 2 * (group % 2)
        some = total[group] > 0
        whole = jnp.where(some, total[group], 1.0)
        level = jnp.where(some, top[group] * RATE + jnp.log2(whole), LOW)
        result = (acc[group] * jnp.where(some, 1.0 / whole, 0.0)).astype(jnp.bfloat16)
        high = level.astype(jnp.bfloat16)
        rest = level - high.astype(jnp.float32)
        middle = rest.astype(jnp.bfloat16)
        low = rest - middle.astype(jnp.float32)
        row = lax.broadcasted_iota(jnp.int32, (EXTRA, WIDE), 0)
        digits = jnp.where(row == 0, high.astype(jnp.float32), jnp.where(row == 1, middle.astype(jnp.float32), low))
        digits = digits.astype(jnp.bfloat16)
        for half in range(2):
            slot = slot_of(first + half)
            lanes, to = slice(half * BLOCK, (half + 1) * BLOCK), slice(i * BLOCK, (i + 1) * BLOCK)
            out_ref[slot, 0:HD, to] = result[:, lanes]
            out_ref[slot, HD:, to] = digits[:, lanes]


def combine_kernel(*refs):
    parts, out_ref = refs[0:4], refs[4]
    levels = []
    for part in parts:
        digits = part[HD:, :].astype(jnp.float32)
        levels.append(digits[0:1] + digits[1:2] + digits[2:3])
    peak = functools.reduce(jnp.maximum, levels)
    shares = [jnp.exp2(level - peak) for level in levels]
    whole = functools.reduce(jnp.add, shares)
    summed = jnp.zeros((HD, 4 * BLOCK), jnp.float32)
    for part, share in zip(parts, shares):
        summed += part[0:HD, :].astype(jnp.float32) * (share / whole)
    out_ref[...] = summed.T.astype(jnp.bfloat16)


def project_kernel(heads_ref, own_ref, beside_ref, out_ref, held):
    zl, tile = at_spot()[0], 2048
    for zh in range(4):
        columns = slice(zh * HD, (zh + 1) * HD)
        held[0, :, columns] = heads_ref[2 * zh + zl]
        held[1, :, columns] = heads_ref[2 * zh + 1 - zl]

    def step(n, carry):
        columns = pl.ds(pl.multiple_of(n * tile, tile), tile)
        product = jnp.dot(held[0], own_ref[:, columns], preferred_element_type=jnp.float32)
        product += jnp.dot(held[1], beside_ref[:, columns], preferred_element_type=jnp.float32)
        out_ref[:, columns] = product.astype(jnp.bfloat16)
        return carry

    lax.fori_loop(0, out_ref.shape[1] // tile, step, 0)


def vmem(n):
    return [pl.BlockSpec(memory_space=pltpu.VMEM)] * n


def attend(queries, keys_values):
    block = (SPARE + 1, BLOCK, HD)
    row = (GROUPS + 1, 1, WIDE)
    return pl.pallas_call(
        attention_kernel,
        out_shape=jax.ShapeDtypeStruct((4, HD + EXTRA, 4 * BLOCK), jnp.bfloat16),
        in_specs=vmem(8),
        out_specs=vmem(1)[0],
        scratch_shapes=[
            pltpu.VMEM((GROUPS // 2 + 1, 4 * BLOCK, HD), jnp.bfloat16),
            pltpu.VMEM(block, jnp.bfloat16),
            pltpu.VMEM(block, jnp.bfloat16),
            pltpu.VMEM(block, jnp.uint32),
            pltpu.VMEM(row, jnp.uint32),
            pltpu.VMEM(row, jnp.float32),
            pltpu.VMEM(row, jnp.float32),
            pltpu.VMEM((GROUPS + 1, HD, WIDE), jnp.float32),
            pltpu.VMEM((WIDE, WIDE), jnp.float32),
            pltpu.VMEM((WIDE, WIDE), jnp.float32),
            pltpu.VMEM((WIDE, WIDE), jnp.bfloat16),
            pltpu.VMEM((WIDE, WIDE), jnp.bfloat16),
            pltpu.VMEM((1, WIDE), jnp.float32),
            pltpu.VMEM((1, WIDE), jnp.float32),
            pltpu.VMEM((1, WIDE), jnp.float32),
            pltpu.VMEM((1, WIDE), jnp.float32),
            pltpu.SMEM((192,), jnp.int32),
            pltpu.SMEM((96,), jnp.int32),
            pltpu.VMEM((32, HD), jnp.int32),
            pltpu.SMEM((32, HD), jnp.int32),
            pltpu.SemaphoreType.DMA,
        ],
        compiler_params=pltpu.CompilerParams(vmem_limit_bytes=10 * 1024 * 1024),
    )(*queries, *keys_values)


def combine(pieces):
    return pl.pallas_call(
        combine_kernel,
        out_shape=jax.ShapeDtypeStruct((4 * BLOCK, HD), jnp.bfloat16),
        in_specs=vmem(4),
        out_specs=vmem(1)[0],
        compiler_params=pltpu.CompilerParams(vmem_limit_bytes=8 * 1024 * 1024),
    )(*pieces)


def project(heads, own, beside):
    return pl.pallas_call(
        project_kernel,
        out_shape=jax.ShapeDtypeStruct((PART, own.shape[1]), jnp.bfloat16),
        in_specs=vmem(3),
        out_specs=vmem(1)[0],
        scratch_shapes=[pltpu.VMEM((2, PART, 4 * HD), jnp.bfloat16)],
        compiler_params=pltpu.CompilerParams(vmem_limit_bytes=10 * 1024 * 1024),
    )(heads, own, beside)


def body(query, key_in, value, doc_ids, out_weight):
    core = lax.axis_index("core").astype(jnp.int32)

    def heads_of(array, c):
        array = array.reshape(HALF, 2, 2, 4, HD)
        array = lax.dynamic_index_in_dim(array, c, 2, keepdims=False)
        return array.transpose(2, 1, 0, 3).reshape(8, HALF, HD)

    mine = [heads_of(a, core) for a in (query, key_in, value)]
    theirs = jnp.stack([heads_of(a, 1 - core) for a in (query, key_in, value)], axis=1)
    theirs = permute(theirs, ("core",), lambda at: {"core": at["core"] + 1})
    marks = jnp.arange(8, dtype=jnp.int32)
    counts = jnp.sum((doc_ids[None, :] < marks[:, None]).astype(jnp.float32), axis=1).astype(jnp.bfloat16)
    extra = jnp.broadcast_to(jnp.pad(counts, (0, HD - 8)), (8, EXTRA // 2, HD))
    sent = jnp.concatenate(
        [mine[0], theirs[:, 0], mine[1], theirs[:, 1], mine[2], theirs[:, 2], extra], axis=1
    )
    held = lax.all_to_all(sent, ("zh", "zl"), 0, 0, tiled=True)
    held, weight = lax.optimization_barrier((held, out_weight))

    def next_chip(at):
        z = (2 * at["zh"] + at["zl"] + (1 if at["core"] == 0 else -1)) % 8
        return {"zh": z // 2, "zl": z % 2}

    beside = permute(weight, ("zl", "core", "zh"), next_chip)
    extra = jnp.concatenate([held[:, 3 * PART :]] * 2, axis=1)
    own_q = jnp.concatenate([held[:, :PART], extra], axis=1)
    own_kv = jnp.concatenate([extra, held[:, PART : 3 * PART]], axis=1)
    after, before = ring(own_kv, "y", -1), ring(own_kv, "y", 1)
    keys_values = [own_kv, after, ring(after, "y", -1), before]
    q_before = ring(own_q, "x", 1)
    queries = [own_q, ring(own_q, "x", -1), ring(q_before, "x", 1), q_before]
    pieces = attend(queries, keys_values)
    pieces = [pieces[0]] + [ring(pieces[s], "x", OFFSETS[s]) for s in (1, 3, 2)]
    attended = combine(pieces).reshape(8, PART, HD)
    heads = lax.all_to_all(attended, ("zh", "zl"), 0, 0, tiled=True)
    mixed = project(heads, out_weight, beside)
    other = permute(mixed[HALF:], ("core",), lambda at: {"core": at["core"] + 1})
    return (mixed[:HALF].astype(jnp.float32) + other.astype(jnp.float32)).astype(jnp.bfloat16)[None]


def solution(mesh):
    apart = Mesh(mesh.devices.reshape(tuple(SIZES.values())), AXES)
    block, head = ("zh", "y", "x"), ("zl", "core")
    array = P(block, head, None, None)
    return jax.shard_map(
        body,
        mesh=apart,
        in_specs=(array, array, array, P(block), P(head, None)),
        out_specs=P(block, head, None),
        check_vma=False,
    )
```

```python
import functools
import itertools
import math

import jax
import jax.numpy as jnp
from jax import lax
from jax.experimental import pallas as pl
from jax.experimental.pallas import tpu as pltpu
from jax.sharding import Mesh
from jax.sharding import PartitionSpec as P

SIZES = {"zl": 2, "core": 2, "zh": 4, "y": 4, "x": 4}
AXES = tuple(SIZES)
BLOCK = 192
PART = 96
HALF = 48
HD = 128
EXTRA = 16
OFFSETS = (0, 1, 2, -1)
LOW = -1e30
MASKED = -2e30
SPAN = 1 << 14
WIDE = 2 * BLOCK
GROUPS = 8
SPARE = 16
RATE = math.log2(math.e) / math.sqrt(HD)


def permute(array, axes, move):
    axes = [a for a in AXES if a in axes]

    def index(at):
        return functools.reduce(lambda n, a: n * SIZES[a] + at[a] % SIZES[a], axes, 0)

    pairs = []
    for spot in itertools.product(*[range(SIZES[a]) for a in axes]):
        at = dict(zip(axes, spot))
        pairs.append((index(at), index({**at, **move(at)})))
    return lax.ppermute(array, tuple(axes), pairs)


def ring(array, first, step):
    second = "y" if first == "x" else "x"

    def move(at):
        axis = first if at["core"] == 0 else second
        return {axis: at[axis] + step}

    return permute(array, ("core", "y", "x"), move)


def at_spot():
    return [lax.axis_index(a).astype(jnp.int32) for a in AXES]


def attention_kernel(*refs):
    q_refs, kv_refs, out_ref = refs[0:4], refs[4:8], refs[8]
    q_all, k_all, v_all, k_code, q_code, top, total, acc = refs[9:17]
    scores_of, weights_of, keep_of, peak_of = refs[17:19], refs[19:21], refs[21:23], refs[23:25]
    tile_keys, tile_group, table, plan, sent = refs[25:30]
    _, swap, _, y, x = at_spot()
    mine = jnp.where(swap == 0, x, y)
    theirs = jnp.where(swap == 0, y, x)

    def place(row):
        odd = lax.rem(row // HALF, 2)
        return row + swap * HALF * (1 - 2 * odd)

    def slot_of(at):
        return lax.rem(at - mine + 4, 4)

    def q_base(at):
        return jnp.where(swap == 0, 4 * y + at, 4 * at + x)

    def k_base(at):
        return jnp.where(swap == 0, 4 * at + x, 4 * y + at)

    for s in range(4):
        for i in range(4):
            n = 4 * s + i
            q_row = q_refs[s][2 * i, PART : PART + EXTRA, :].astype(jnp.float32)
            k_row = kv_refs[s][2 * i, 0:EXTRA, :].astype(jnp.float32)
            table[n : n + 1, :] = q_row[0:1].astype(jnp.int32)
            table[16 + n : 17 + n, :] = k_row[0:1].astype(jnp.int32)
    counts = table[...]
    row = lax.broadcasted_iota(jnp.int32, counts.shape, 0)
    lane = lax.broadcasted_iota(jnp.int32, counts.shape, 1)

    def tally(mask, axis):
        return jnp.sum(jnp.where(mask, 1.0, 0.0), axis=axis, keepdims=True)

    inner = (lane >= 1) & (lane < 8)
    first, last = tally(inner & (counts == 0), 1), tally(inner & (counts < BLOCK), 1)
    k_last = jnp.sum(jnp.where(row == lane + 16, last, 0.0), axis=0, keepdims=True)
    q_at = q_base(lax.rem(mine + row // 4, 4)) + 16 * lax.rem(row, 4)
    k_at = k_base(lax.rem(theirs + lane // 4, 4)) + 16 * lax.rem(lane, 4)
    some = (q_at >= k_at) & (k_last >= first) & (lane < 16)
    bits = jnp.sum(jnp.where(some, lax.shift_left(1, jnp.minimum(lane, 16)).astype(jnp.float32), 0.0), axis=1, keepdims=True)
    for at, column in ((8, first), (9, last), (10, bits)):
        counts = jnp.where(lane == at, column.astype(jnp.int32), counts)
    table[...] = counts
    copy = pltpu.make_async_copy(table, plan, sent)
    copy.start()

    for s in range(4):
        at = lax.rem(mine + s, 4) * BLOCK
        for z in range(8):
            i, row = z // 2, (z % 2) * PART
            to = pl.multiple_of(at + row, PART)
            q_all[i, pl.ds(to, PART), :] = q_refs[s][z, 0:PART, :]
            k_all[4 * s + i, row : row + PART, :] = kv_refs[s][z, EXTRA : EXTRA + PART, :]
            v_all[4 * s + i, row : row + PART, :] = kv_refs[s][z, EXTRA + PART :, :]
    k_all[SPARE] = jnp.zeros((BLOCK, HD), jnp.bfloat16)
    v_all[SPARE] = jnp.zeros((BLOCK, HD), jnp.bfloat16)
    top[...] = jnp.full_like(top, LOW)
    total[...] = jnp.zeros_like(total)
    acc[...] = jnp.zeros_like(acc)
    copy.wait()

    def clear(n):
        tile_keys[2 * n] = SPARE
        tile_keys[2 * n + 1] = SPARE
        tile_group[n] = GROUPS

    clear(0)
    clear(1)
    end = jnp.int32(4)
    for group in range(GROUPS):
        i, first = group // 2, 2 * (group % 2)
        bits = plan[4 * slot_of(first) + i, 10] | plan[4 * slot_of(first + 1) + i, 10]
        for slot in range(4):
            for j in range(i + 1):
                kb = 4 * slot + j
                tile_keys[end] = kb
                tile_group[end // 2] = group
                end = end + (lax.shift_right_logical(bits, kb) & 1)
        tile_keys[end] = SPARE
        end = ((end + 1) // 2) * 2
    tiles = end // 2
    for n in range(4):
        clear(tiles + n)

    row_place = place(lax.broadcasted_iota(jnp.int32, (BLOCK, HD), 0))
    for kb in range(16):
        base = (k_base(lax.rem(theirs + kb // 4, 4)) + 16 * (kb % 4)) * BLOCK
        first, last = plan[16 + kb, 8], plan[16 + kb, 9]
        k_code[kb] = (row_place + (base + first * SPAN)).astype(jnp.uint32)

        def add(d, carry, kb=kb):
            k_code[kb] += jnp.where(plan[16 + kb, d] <= row_place, SPAN, 0).astype(jnp.uint32)
            return carry

        lax.fori_loop(first + 1, last + 1, add, 0)
    k_code[SPARE] = jnp.full((BLOCK, HD), 1 << 30, jnp.uint32)
    lane = lax.broadcasted_iota(jnp.int32, (1, WIDE), 1)
    second = lane >= BLOCK
    lane_place = place(jnp.where(second, lane - BLOCK, lane))
    for group in range(GROUPS):
        i, first = group // 2, 2 * (group % 2)
        slots = [slot_of(first), slot_of(first + 1)]
        code = lane_place + jnp.where(second, q_base(first + 1), q_base(first)) * BLOCK + 16 * i * BLOCK
        for d in range(1, 8):
            counts = [plan[4 * slot + i, d] for slot in slots]
            code += jnp.where(jnp.where(second, counts[1], counts[0]) <= lane_place, SPAN, 0)
        q_code[group] = code.astype(jnp.uint32)
    q_code[GROUPS] = jnp.zeros((1, WIDE), jnp.uint32)

    def stage(n, odd):
        group = tile_group[n + 2]
        row = pl.multiple_of(lax.rem(group, 2) * WIDE, WIDE)
        queries = q_all[group // 2, pl.ds(row, WIDE), :]
        q_row = q_code[group]
        peaks = []
        for half in range(2):
            kb = tile_keys[2 * n + 4 + half]
            scores = lax.dot_general(
                k_all[kb], queries, (((1,), (1,)), ((), ())), preferred_element_type=jnp.float32
            )
            ahead = q_row - jnp.concatenate([k_code[kb]] * (WIDE // HD), axis=1)
            scores = jnp.where(ahead < SPAN, scores, MASKED)
            scores_of[odd][half * BLOCK : (half + 1) * BLOCK, :] = scores
            peaks.append(jnp.max(scores, axis=0, keepdims=True))
        peak_of[odd][...] = jnp.maximum(peaks[0], peaks[1])

        group = tile_group[n + 1]
        old = top[group]
        new = jnp.maximum(old, peak_of[1 - odd][...])
        keep = jnp.exp2((old - new) * RATE)
        top[group] = new
        keep_of[1 - odd][...] = keep
        weights = jnp.exp2((scores_of[1 - odd][...] - new) * RATE)
        total[group] = total[group] * keep + jnp.sum(weights, axis=0, keepdims=True)
        weights_of[1 - odd][...] = weights.astype(jnp.bfloat16)

        group = tile_group[n]
        product = acc[group] * keep_of[odd][...]
        for half in range(2):
            product += lax.dot_general(
                v_all[tile_keys[2 * n + half]],
                weights_of[odd][half * BLOCK : (half + 1) * BLOCK, :],
                (((0,), (0,)), ((), ())),
                preferred_element_type=jnp.float32,
            )
        acc[group] = product

    def step(n, carry):
        stage(2 * n, 0)
        stage(2 * n + 1, 1)
        return carry

    lax.fori_loop(0, (tiles + 1) // 2, step, 0)

    for group in range(GROUPS):
        i, first = group // 2, 2 * (group % 2)
        some = total[group] > 0
        whole = jnp.where(some, total[group], 1.0)
        level = jnp.where(some, top[group] * RATE + jnp.log2(whole), LOW)
        result = (acc[group] * jnp.where(some, 1.0 / whole, 0.0)).astype(jnp.bfloat16)
        high = level.astype(jnp.bfloat16)
        rest = level - high.astype(jnp.float32)
        middle = rest.astype(jnp.bfloat16)
        low = rest - middle.astype(jnp.float32)
        row = lax.broadcasted_iota(jnp.int32, (EXTRA, WIDE), 0)
        digits = jnp.where(row == 0, high.astype(jnp.float32), jnp.where(row == 1, middle.astype(jnp.float32), low))
        digits = digits.astype(jnp.bfloat16)
        for half in range(2):
            slot = slot_of(first + half)
            lanes, to = slice(half * BLOCK, (half + 1) * BLOCK), slice(i * BLOCK, (i + 1) * BLOCK)
            out_ref[slot, 0:HD, to] = result[:, lanes]
            out_ref[slot, HD:, to] = digits[:, lanes]


def combine_kernel(*refs):
    parts, out_ref = refs[0:4], refs[4]
    levels = []
    for part in parts:
        digits = part[HD:, :].astype(jnp.float32)
        levels.append(digits[0:1] + digits[1:2] + digits[2:3])
    peak = functools.reduce(jnp.maximum, levels)
    shares = [jnp.exp2(level - peak) for level in levels]
    whole = functools.reduce(jnp.add, shares)
    summed = jnp.zeros((HD, 4 * BLOCK), jnp.float32)
    for part, share in zip(parts, shares):
        summed += part[0:HD, :].astype(jnp.float32) * (share / whole)
    out_ref[...] = summed.T.astype(jnp.bfloat16)


def project_kernel(heads_ref, own_ref, beside_ref, out_ref, held):
    zl, tile = at_spot()[0], 4096
    for zh in range(4):
        columns = slice(zh * HD, (zh + 1) * HD)
        held[0, :, columns] = heads_ref[2 * zh + zl]
        held[1, :, columns] = heads_ref[2 * zh + 1 - zl]

    def step(n, carry):
        columns = pl.ds(pl.multiple_of(n * tile, tile), tile)
        product = jnp.dot(held[0], own_ref[:, columns], preferred_element_type=jnp.float32)
        product += jnp.dot(held[1], beside_ref[:, columns], preferred_element_type=jnp.float32)
        out_ref[:, columns] = product.astype(jnp.bfloat16)
        return carry

    lax.fori_loop(0, out_ref.shape[1] // tile, step, 0)


def vmem(n):
    return [pl.BlockSpec(memory_space=pltpu.VMEM)] * n


def attend(queries, keys_values):
    block = (SPARE + 1, BLOCK, HD)
    row = (GROUPS + 1, 1, WIDE)
    return pl.pallas_call(
        attention_kernel,
        out_shape=jax.ShapeDtypeStruct((4, HD + EXTRA, 4 * BLOCK), jnp.bfloat16),
        in_specs=vmem(8),
        out_specs=vmem(1)[0],
        scratch_shapes=[
            pltpu.VMEM((GROUPS // 2 + 1, 4 * BLOCK, HD), jnp.bfloat16),
            pltpu.VMEM(block, jnp.bfloat16),
            pltpu.VMEM(block, jnp.bfloat16),
            pltpu.VMEM(block, jnp.uint32),
            pltpu.VMEM(row, jnp.uint32),
            pltpu.VMEM(row, jnp.float32),
            pltpu.VMEM(row, jnp.float32),
            pltpu.VMEM((GROUPS + 1, HD, WIDE), jnp.float32),
            pltpu.VMEM((WIDE, WIDE), jnp.float32),
            pltpu.VMEM((WIDE, WIDE), jnp.float32),
            pltpu.VMEM((WIDE, WIDE), jnp.bfloat16),
            pltpu.VMEM((WIDE, WIDE), jnp.bfloat16),
            pltpu.VMEM((1, WIDE), jnp.float32),
            pltpu.VMEM((1, WIDE), jnp.float32),
            pltpu.VMEM((1, WIDE), jnp.float32),
            pltpu.VMEM((1, WIDE), jnp.float32),
            pltpu.SMEM((192,), jnp.int32),
            pltpu.SMEM((96,), jnp.int32),
            pltpu.VMEM((32, HD), jnp.int32),
            pltpu.SMEM((32, HD), jnp.int32),
            pltpu.SemaphoreType.DMA,
        ],
        compiler_params=pltpu.CompilerParams(vmem_limit_bytes=10 * 1024 * 1024),
    )(*queries, *keys_values)


def combine(pieces):
    return pl.pallas_call(
        combine_kernel,
        out_shape=jax.ShapeDtypeStruct((4 * BLOCK, HD), jnp.bfloat16),
        in_specs=vmem(4),
        out_specs=vmem(1)[0],
        compiler_params=pltpu.CompilerParams(vmem_limit_bytes=8 * 1024 * 1024),
    )(*pieces)


def project(heads, own, beside):
    return pl.pallas_call(
        project_kernel,
        out_shape=jax.ShapeDtypeStruct((PART, own.shape[1]), jnp.bfloat16),
        in_specs=vmem(3),
        out_specs=vmem(1)[0],
        scratch_shapes=[pltpu.VMEM((2, PART, 4 * HD), jnp.bfloat16)],
        compiler_params=pltpu.CompilerParams(vmem_limit_bytes=14 * 1024 * 1024),
    )(heads, own, beside)


def body(query, key_in, value, doc_ids, out_weight):
    core = lax.axis_index("core").astype(jnp.int32)

    def heads_of(array, c):
        array = array.reshape(HALF, 2, 2, 4, HD)
        array = lax.dynamic_index_in_dim(array, c, 2, keepdims=False)
        return array.transpose(2, 1, 0, 3).reshape(8, HALF, HD)

    mine = [heads_of(a, core) for a in (query, key_in, value)]
    theirs = jnp.stack([heads_of(a, 1 - core) for a in (query, key_in, value)], axis=1)
    theirs = permute(theirs, ("core",), lambda at: {"core": at["core"] + 1})
    marks = jnp.arange(8, dtype=jnp.int32)
    counts = jnp.sum((doc_ids[None, :] < marks[:, None]).astype(jnp.float32), axis=1).astype(jnp.bfloat16)
    extra = jnp.broadcast_to(jnp.pad(counts, (0, HD - 8)), (8, EXTRA // 2, HD))
    sent = jnp.concatenate(
        [mine[0], theirs[:, 0], mine[1], theirs[:, 1], mine[2], theirs[:, 2], extra], axis=1
    )
    held = lax.all_to_all(sent, ("zh", "zl"), 0, 0, tiled=True)
    held, weight = lax.optimization_barrier((held, out_weight))

    def next_chip(at):
        z = (2 * at["zh"] + at["zl"] + (1 if at["core"] == 1 else -1)) % 8
        return {"zh": z // 2, "zl": z % 2}

    beside = permute(weight, ("zl", "core", "zh"), next_chip)
    extra = jnp.concatenate([held[:, 3 * PART :]] * 2, axis=1)
    own_q = jnp.concatenate([held[:, :PART], extra], axis=1)
    own_kv = jnp.concatenate([extra, held[:, PART : 3 * PART]], axis=1)
    after, before = ring(own_kv, "y", -1), ring(own_kv, "y", 1)
    keys_values = [own_kv, after, ring(after, "y", -1), before]
    q_before = ring(own_q, "x", 1)
    queries = [own_q, ring(own_q, "x", -1), ring(q_before, "x", 1), q_before]
    pieces = attend(queries, keys_values)
    pieces = [pieces[0]] + [ring(pieces[s], "x", OFFSETS[s]) for s in (1, 3, 2)]
    attended = combine(pieces).reshape(8, PART, HD)
    heads = lax.all_to_all(attended, ("zh", "zl"), 0, 0, tiled=True)
    mixed = project(heads, out_weight, beside)
    other = permute(mixed[HALF:], ("core",), lambda at: {"core": at["core"] + 1})
    return (mixed[:HALF].astype(jnp.float32) + other.astype(jnp.float32)).astype(jnp.bfloat16)[None]


def solution(mesh):
    apart = Mesh(mesh.devices.reshape(tuple(SIZES.values())), AXES)
    block, head = ("zh", "y", "x"), ("zl", "core")
    array = P(block, head, None, None)
    return jax.shard_map(
        body,
        mesh=apart,
        in_specs=(array, array, array, P(block), P(head, None)),
        out_specs=P(block, head, None),
        check_vma=False,
    )
```
